1024 devices in a mesh: rep: 8 (over y), outer: 16 (over z), inner: 8 (over x, core).
Axes of the slice: x: 4, y: 8, z: 16, core: 2. Of those that a mesh axis runs over, the one named last changes fastest.
Arguments:
- tokens: bfloat16 [16384, 1024], P(('outer', 'inner')), may hold values from -6 to 6
- cotangent: bfloat16 [16384, 1024], P(('outer', 'inner')), may hold values from -6 to 6
- routes: int32 [16384, 8], P(('outer', 'inner'), 'rep'), may hold values from 0 to 127, as said below
- gate_weights: float32 [16384, 8], P(('outer', 'inner'), 'rep'), may hold values from 0.05 to 0.5
- w_gate: bfloat16 [128, 1024, 384], P(('outer', 'inner')), may hold values from -0.1875 to 0.1875
- w_up: bfloat16 [128, 1024, 384], P(('outer', 'inner')), may hold values from -0.1875 to 0.1875
- w_down: bfloat16 [128, 384, 1024], P(('outer', 'inner')), may hold values from -0.3125 to 0.3125
Outputs:
- combined: bfloat16 [16384, 1024], P(('outer', 'inner'), 'rep')
- grad_tokens: bfloat16 [16384, 1024], P(('outer', 'inner'), 'rep')
- grad_w_gate: bfloat16 [128, 1024, 384], P(('outer', 'inner'), 'rep')
- grad_w_up: bfloat16 [128, 1024, 384], P(('outer', 'inner'), 'rep')
- grad_w_down: bfloat16 [128, 384, 1024], P(('outer', 'inner'), 'rep')
The draws below stay inside these ranges and needn't reach their ends.
Inputs may be any that keep to these rules, and one draw needn't show every extreme that they name: `routes`: each row names 8 different experts. The columns fall into 8 groups of 1 column; within one group and one aligned block of 128 rows no expert is named more than 2 times, and in every block and group some expert is named exactly 2 times.
All inputs are finite; a program needn't handle non-finite values.
Results may differ from the reference program's by a relative error of at most 0.019.
Values may be sent and summed in bfloat16 or wider, within the bound.
A program may use at most 32 MiB of HBM per device.

```python
import math
import jax
import jax.numpy as jnp
from jax import lax

D = 1024
F = 384
TOPK = 8
TOK_DEV = 128
EXPERTS = 128
CAP = 2
TOKENS = 16384
N_REP = 8
N_OUTER = 16
N_INNER = 8


def draw_routes(key, part):
    key = jax.random.fold_in(key, 11)
    blocks = N_OUTER * N_INNER
    route_share = TOPK // N_REP
    bases = EXPERTS // route_share
    slot_count = bases * CAP

    def one_block(block_key):
        keys = jax.random.split(block_key, 5)
        slot_value = jnp.arange(slot_count, dtype=jnp.int32) // CAP
        popular = jax.random.randint(keys[0], (bases,), 0, 2 ** 15, dtype=jnp.int32)
        noise = jax.random.randint(keys[1], (slot_count,), 0, 2 ** 15, dtype=jnp.int32)
        chosen = jax.random.randint(keys[2], (), 0, bases, dtype=jnp.int32)
        score = jnp.where(slot_value == chosen, 2 ** 17, noise + popular[slot_value])
        score = score * slot_count + jnp.arange(slot_count, dtype=jnp.int32)
        unused, picked = lax.top_k(score, TOK_DEV)
        base_ids = jax.random.permutation(keys[3], slot_value[picked])
        relabel = jax.random.permutation(keys[4], EXPERTS).astype(jnp.int32)
        columns = jnp.arange(TOPK, dtype=jnp.int32)
        return relabel[(route_share * base_ids[:, None] + columns[None, :]) % EXPERTS]
    block_keys = jax.random.split(key, blocks)
    return jax.vmap(one_block)(block_keys).reshape(TOK_DEV * blocks, TOPK).astype(jnp.int32)


def shard_levels(rng, shape, cuts, low, high):
    loudness = 1.0
    for dim, parts in cuts:
        steps = jax.random.uniform(jax.random.fold_in(jax.random.fold_in(rng, 6), dim), (parts,), jnp.float32, low / len(cuts), high / len(cuts))
        loudness = loudness * jnp.repeat(jnp.exp(steps), shape[dim] // parts).reshape((-1,) + (1,) * (len(shape) - 1 - dim))
    return loudness


def centred(key, shape, width, reach, shards=(), kind=jnp.bfloat16):
    entries = width * jax.random.normal(key, shape, jnp.float32)
    if shards:
        entries = entries * shard_levels(key, shape, shards, -0.22, 0.18)
    return jnp.clip(entries, -reach, reach).astype(kind)


def setup_inputs(seed: int = 0) -> dict:
    splits = jax.random.split(jax.random.key(seed), 8)
    return {
        "tokens": centred(splits[0], (TOKENS, D), 1.0, 6.0, ((0, 128),)),
        "cotangent": centred(splits[1], (TOKENS, D), 1.0, 6.0, ((0, 128),)),
        "routes": draw_routes(jax.random.fold_in(splits[7], 71), 0),
        "gate_weights": jnp.clip(jnp.exp(math.log(0.5) - 2.3025851 * jax.random.uniform(splits[3], (TOKENS, TOPK), jnp.float32) ** shard_levels(splits[3], (TOKENS, TOPK), ((0, 128), (1, 8)), -0.2, 0.2)), 0.05, 0.5),
        "w_gate": centred(splits[4], (EXPERTS, D, F), D ** -0.5, 0.1875, ((0, 128),)),
        "w_up": centred(splits[5], (EXPERTS, D, F), D ** -0.5, 0.1875, ((0, 128),)),
        "w_down": centred(splits[6], (EXPERTS, F, D), F ** -0.5, 0.3125, ((0, 128),)),
    }


def expert_math(tok_slots, scaled_in, gate_f32, up_f32, down_f32):
    high = lax.Precision.HIGHEST
    tok_wide = tok_slots.astype(jnp.float32)
    scaled_wide = scaled_in.astype(jnp.float32)
    gate_pre = jnp.einsum("erd,edf->erf", tok_wide, gate_f32, precision=high)
    up_pre = jnp.einsum("erd,edf->erf", tok_wide, up_f32, precision=high)
    sigmoid_gate = jax.nn.sigmoid(gate_pre)
    silu_gate = gate_pre * sigmoid_gate
    hidden = (silu_gate * up_pre).astype(jnp.bfloat16)
    hidden_wide = hidden.astype(jnp.float32)
    expert_out = jnp.einsum("erf,efd->erd", hidden_wide, down_f32, precision=high).astype(jnp.bfloat16)
    hidden_grad = jnp.einsum("erd,efd->erf", scaled_wide, down_f32, precision=high)
    gate_grad = (hidden_grad * up_pre * sigmoid_gate * (1.0 + gate_pre * (1.0 - sigmoid_gate))).astype(jnp.bfloat16)
    up_grad = (hidden_grad * silu_gate).astype(jnp.bfloat16)
    gate_grad_wide = gate_grad.astype(jnp.float32)
    up_grad_wide = up_grad.astype(jnp.float32)
    pair_grad = (jnp.einsum("erf,edf->erd", gate_grad_wide, gate_f32, precision=high)
                 + jnp.einsum("erf,edf->erd", up_grad_wide, up_f32, precision=high)).astype(jnp.bfloat16)
    grad_gate = jnp.einsum("erd,erf->edf", tok_wide, gate_grad_wide, precision=high)
    grad_up = jnp.einsum("erd,erf->edf", tok_wide, up_grad_wide, precision=high)
    grad_down = jnp.einsum("erf,erd->efd", hidden_wide, scaled_wide, precision=high)
    return expert_out, pair_grad, grad_gate, grad_up, grad_down


def rounded(value):
    return lax.optimization_barrier(value.astype(jnp.bfloat16)).astype(jnp.float32)


def reference(tokens, cotangent, routes, gate_weights, w_gate, w_up, w_down):
    blocks = N_OUTER * N_INNER
    route_share = TOPK // N_REP
    pair_count = TOK_DEV * route_share
    slot_rows = blocks * CAP
    gate_f32 = w_gate.astype(jnp.float32)
    up_f32 = w_up.astype(jnp.float32)
    down_f32 = w_down.astype(jnp.float32)
    tok_blocks = tokens.reshape(blocks, TOK_DEV, D)
    cot_blocks = cotangent.reshape(blocks, TOK_DEV, D)
    tok_pairs = jnp.repeat(tok_blocks, route_share, axis=1)
    cot_pairs = jnp.repeat(cot_blocks, route_share, axis=1).astype(jnp.float32)
    route_groups = routes.astype(jnp.int32).reshape(blocks, TOK_DEV, N_REP, route_share)
    route_groups = route_groups.transpose(2, 0, 1, 3).reshape(N_REP, blocks, pair_count)
    gate_groups = gate_weights.reshape(blocks, TOK_DEV, N_REP, route_share)
    gate_groups = gate_groups.transpose(2, 0, 1, 3).reshape(N_REP, blocks, pair_count)
    positions = jnp.arange(pair_count, dtype=jnp.int32)
    lower_mask = positions[:, None] > positions[None, :]

    def group_step(totals, pieces):
        route_ids, gate_vals = pieces
        same = route_ids[:, :, None] == route_ids[:, None, :]
        slot_rank = jnp.sum(same & lower_mask[None], axis=2).astype(jnp.int32)
        buffer_rows = (jnp.arange(blocks, dtype=jnp.int32)[:, None] * CAP + slot_rank).astype(jnp.int32)
        scaled_pairs = (gate_vals[:, :, None] * cot_pairs).astype(jnp.bfloat16)
        tok_slots = jnp.zeros((EXPERTS, slot_rows, D), tok_pairs.dtype).at[route_ids, buffer_rows].set(tok_pairs)
        scaled_in = jnp.zeros((EXPERTS, slot_rows, D), scaled_pairs.dtype).at[route_ids, buffer_rows].set(scaled_pairs)
        expert_out, pair_grad, grad_gate, grad_up, grad_down = expert_math(tok_slots, scaled_in, gate_f32, up_f32, down_f32)
        picked = expert_out[route_ids, buffer_rows].reshape(blocks, TOK_DEV, route_share, D).astype(jnp.float32)
        picked_grad = pair_grad[route_ids, buffer_rows].reshape(blocks, TOK_DEV, route_share, D).astype(jnp.float32)
        weights = gate_vals.reshape(blocks, TOK_DEV, route_share)
        combined = totals[0] + jnp.sum(weights[..., None] * picked, axis=2)
        token_grads = totals[1] + jnp.sum(picked_grad, axis=2)
        return (combined, token_grads, totals[2] + rounded(grad_gate), totals[3] + rounded(grad_up),
                totals[4] + rounded(grad_down)), None

    start = (jnp.zeros((blocks, TOK_DEV, D), jnp.float32), jnp.zeros((blocks, TOK_DEV, D), jnp.float32),
             jnp.zeros((EXPERTS, D, F), jnp.float32), jnp.zeros((EXPERTS, D, F), jnp.float32),
             jnp.zeros((EXPERTS, F, D), jnp.float32))
    summed, unused = lax.scan(group_step, start, (route_groups, gate_groups))
    return (summed[0].reshape(TOKENS, D).astype(jnp.bfloat16), summed[1].reshape(TOKENS, D).astype(jnp.bfloat16),
            summed[2].astype(jnp.bfloat16), summed[3].astype(jnp.bfloat16), summed[4].astype(jnp.bfloat16))
```

```python
import functools

import jax
import jax.numpy as jnp
from jax import lax
from jax.experimental import pallas as pl
from jax.experimental.pallas import tpu as pltpu
from jax.sharding import PartitionSpec as P

MESH = pl.DeviceIdType.MESH
LANES = 128
F32 = jnp.float32
BF16 = jnp.bfloat16


def dot(a, b, dims=((1,), (0,))):
    return lax.dot_general(a, b, (dims, ((), ())), preferred_element_type=F32)


def kernel(
    sizes,
    tok_ref, cot_ref, routes_ref, gate_ref, wg_hbm, wu_hbm, wd_hbm,
    comb_ref, gtok_ref, gg_ref, gu_ref, gd_ref,
    wg, wu, wd, wide, send, recv, tok_in, sc_in, gpre, upre, hid, both,
    own_gu, own_dn, got_gu, got_dn, put_gu, put_dn, part, parts_in,
    w_sem, a2a_send, a2a_recv, ch_send, ch_recv, rep_send, rep_recv,
):
    n_rep, n_out, n_in, cap = sizes
    peers = n_out * n_in
    rows, width = tok_ref.shape
    blocks = width // LANES
    slots = peers * cap
    half = n_rep // 2
    r, o, i = lax.axis_index("rep"), lax.axis_index("outer"), lax.axis_index("inner")
    me = o * n_in + i

    barrier = pltpu.get_barrier_semaphore()

    def greet(k, c):
        o2, i2 = lax.rem(o + lax.div(k, n_in), n_out), lax.rem(i + lax.rem(k, n_in), n_in)
        pl.semaphore_signal(barrier, inc=1, device_id=(r, o2, i2), device_id_type=MESH)
        return c

    def greet_rep(k, c):
        pl.semaphore_signal(
            barrier, inc=1, device_id=(lax.rem(r + k, n_rep), o, i), device_id_type=MESH
        )
        return c

    lax.fori_loop(1, peers, greet, 0)
    lax.fori_loop(1, n_rep, greet_rep, 0)

    loads = [
        pltpu.make_async_copy(src, dst, w_sem.at[n])
        for n, (src, dst) in enumerate(((wg_hbm, wg), (wu_hbm, wu), (wd_hbm, wd)))
    ]
    for load in loads:
        load.start()

    ids = routes_ref[...].astype(F32)
    sub = lax.broadcasted_iota(jnp.int32, (rows, rows), 0)
    lane = lax.broadcasted_iota(jnp.int32, (rows, rows), 1)
    ids_row = jnp.sum(jnp.where(sub == lane, ids, 0.0), axis=0, keepdims=True)
    same = ids == ids_row
    rank_col = jnp.sum(jnp.where(same & (sub > lane), 1.0, 0.0), axis=1, keepdims=True)
    rank_row = jnp.sum(jnp.where(same & (sub < lane), 1.0, 0.0), axis=0, keepdims=True)
    slot_col = ids * float(cap) + rank_col
    slot_row = ids_row * float(cap) + rank_row
    place = lax.broadcasted_iota(jnp.int32, (slots, rows), 0).astype(F32)
    to_slots = jnp.where(place == slot_row, 1.0, 0.0).astype(BF16)
    place = lax.broadcasted_iota(jnp.int32, (rows, slots), 1).astype(F32)
    from_slots = jnp.where(place == slot_col, 1.0, 0.0).astype(BF16)
    gates = gate_ref[...]

    def pack(rows_f32, n):
        for c in range(blocks):
            wide[pl.ds(c, slots, stride=blocks), :] = rows_f32[:, c * LANES : (c + 1) * LANES]
        send[n] = wide[...].astype(BF16).reshape(peers, cap * blocks, LANES)
        recv[n, pl.ds(me, 1)] = send[n, pl.ds(me, 1)]

    def exchange(n):
        def one(k, c):
            m, di = lax.div(k, n_in), lax.rem(k, n_in)
            up, odd = lax.div(m + 1, 2), lax.rem(m, 2)
            do = odd * up + (1 - odd) * (n_out - up)
            o2, i2 = lax.rem(o + do, n_out), lax.rem(i + di, n_in)
            pltpu.make_async_remote_copy(
                src_ref=send.at[n, o2 * n_in + i2],
                dst_ref=recv.at[n, me],
                send_sem=a2a_send.at[n],
                recv_sem=a2a_recv.at[n],
                device_id=(r, o2, i2),
                device_id_type=MESH,
            ).start()
            return c

        lax.fori_loop(1, peers, one, 0)

    def arrive(n):
        got = recv.at[n, pl.ds(0, peers - 1)]
        pltpu.make_async_copy(got, got, a2a_recv.at[n]).wait()
        wide[...] = recv[n].reshape(slots * blocks, LANES).astype(F32)

    def block(c):
        return wide[pl.ds(c, slots, stride=blocks), :].astype(BF16)

    def unpack(n, dst):
        arrive(n)
        for c in range(blocks):
            dst[:, c * LANES : (c + 1) * LANES] = block(c)

    pack(dot(to_slots, tok_ref[...]), 0)
    pl.semaphore_wait(barrier, peers - 1 + n_rep - 1)
    exchange(0)
    scaled = (gates * cot_ref[...].astype(F32)).astype(BF16)
    pack(dot(to_slots, scaled), 1)
    exchange(1)

    for load in loads:
        load.wait()
    unpack(0, tok_in)
    gpre[...] = dot(tok_in[...], wg[...])
    upre[...] = dot(tok_in[...], wu[...])
    g = gpre[...]
    hid[...] = (g * jax.nn.sigmoid(g) * upre[...]).astype(BF16)
    pack(dot(hid[...], wd[...]), 2)
    exchange(2)

    unpack(1, sc_in)
    hgrad = dot(sc_in[...], wd[...], ((1,), (1,)))
    g = gpre[...]
    s = jax.nn.sigmoid(g)
    f = g.shape[1]
    both[:, :f] = (hgrad * upre[...] * s * (1.0 + g * (1.0 - s))).astype(BF16)
    both[:, f:] = (hgrad * (g * s)).astype(BF16)
    pack(
        dot(both[:, :f], wg[...], ((1,), (1,))) + dot(both[:, f:], wu[...], ((1,), (1,))), 3
    )
    exchange(3)

    own_gu[...] = dot(tok_in[...], both[...], ((0,), (0,))).astype(BF16).reshape(own_gu.shape)
    own_dn[...] = dot(hid[...], sc_in[...], ((0,), (0,))).astype(BF16).reshape(own_dn.shape)

    pair = ((0, 1, own_gu, got_gu, put_gu), (1, 2, own_dn, got_dn, put_dn))

    def cut(a, side):
        ref = own_gu if a == 0 else own_dn
        if a == 0:
            n = ref.shape[1] // 2
            return (pl.ds(side * n, n), slice(None))
        n = ref.shape[2] // 2
        return (slice(None), pl.ds(side * n, n))

    def hop(a, d, t, src):
        got = pair[a][3]
        dst = got.at[d, t - 1]
        if t == half:
            src, dst = src.at[cut(a, d)], dst.at[cut(a, d)]
        to = lax.rem(r + (1 if d == 0 else n_rep - 1), n_rep)
        return pltpu.make_async_remote_copy(
            src_ref=src,
            dst_ref=dst,
            send_sem=ch_send.at[a, d, t - 1],
            recv_sem=ch_recv.at[a, d, t - 1],
            device_id=(to, o, i),
            device_id_type=MESH,
        )

    def owner(d, t):
        return lax.rem(r + (t if d == 0 else n_rep - t), n_rep)

    hops = {}
    for t in range(half, 0, -1):
        for a, unused, own, got, put in pair:
            for d in range(2):
                j = owner(d, t)
                if t == half:
                    src = own.at[j]
                else:
                    hops[a, d, t + 1].wait_recv()
                    if t + 1 == half:
                        x, y = cut(a, d), cut(a, 1 - d)
                        put[(d, t - 1) + x] = (
                            got[(d, t) + x].astype(F32) + own[(j,) + x].astype(F32)
                        ).astype(BF16)
                        put[(d, t - 1) + y] = own[(j,) + y]
                    else:
                        put[d, t - 1] = (got[d, t].astype(F32) + own[j].astype(F32)).astype(BF16)
                    src = put.at[d, t - 1]
                hops[a, d, t] = hop(a, d, t, src)
                hops[a, d, t].start()
    for a, unused, own, got, put in pair:
        for d in range(2):
            hops[a, d, 1].wait_recv()
        total = own[r].astype(F32) + got[0, 0].astype(F32) + got[1, 0].astype(F32)
        total = total.astype(BF16)
        if a == 0:
            gg_ref[0] = total[:, :f]
            gu_ref[0] = total[:, f:]
        else:
            gd_ref[0] = total

    def share(n, weigh):
        arrive(2 + n)
        for c in range(blocks):
            rows_f32 = dot(from_slots, block(c))
            part[n, c] = (gates * rows_f32 if weigh else rows_f32).astype(BF16)
        parts_in[n, pl.ds(r, 1)] = part[n, pl.ds(r, 1)]

        def one(k, c):
            to = lax.rem(r + k, n_rep)
            pltpu.make_async_remote_copy(
                src_ref=part.at[n, to],
                dst_ref=parts_in.at[n, r],
                send_sem=rep_send.at[n],
                recv_sem=rep_recv.at[n],
                device_id=(to, o, i),
                device_id_type=MESH,
            ).start()
            return c

        lax.fori_loop(1, n_rep, one, 0)

    def collect(n, out):
        got = parts_in.at[n, pl.ds(0, n_rep - 1)]
        pltpu.make_async_copy(got, got, rep_recv.at[n]).wait()
        out[...] = jnp.sum(parts_in[n].astype(F32), axis=0).astype(BF16)

    share(0, True)
    share(1, False)
    collect(0, comb_ref)
    collect(1, gtok_ref)

    for n in range(4):
        sent = send.at[n, pl.ds(0, peers - 1)]
        pltpu.make_async_copy(sent, sent, a2a_send.at[n]).wait()
    for n in range(2):
        sent = part.at[n, pl.ds(0, n_rep - 1)]
        pltpu.make_async_copy(sent, sent, rep_send.at[n]).wait()
    for h in hops.values():
        h.wait_send()


def per_device(tokens, cotangent, routes, gate_weights, w_gate, w_up, w_down):
    n_rep, n_out, n_in = (lax.axis_size(a) for a in ("rep", "outer", "inner"))
    rows, width = tokens.shape
    hidden = w_gate.shape[2]
    peers = n_out * n_in
    cap = max(2, 2 * rows // peers)
    blocks = width // LANES
    slots = peers * cap
    half = n_rep // 2
    own = width // n_rep
    dn = hidden // n_rep
    vmem = pl.BlockSpec(memory_space=pltpu.VMEM)
    hbm = pl.BlockSpec(memory_space=pl.ANY)
    dma = pltpu.SemaphoreType.DMA
    return pl.pallas_call(
        functools.partial(kernel, (n_rep, n_out, n_in, cap)),
        out_shape=(
            jax.ShapeDtypeStruct((rows, own), BF16),
            jax.ShapeDtypeStruct((rows, own), BF16),
            jax.ShapeDtypeStruct((1, own, hidden), BF16),
            jax.ShapeDtypeStruct((1, own, hidden), BF16),
            jax.ShapeDtypeStruct((1, dn, width), BF16),
        ),
        in_specs=[vmem] * 4 + [hbm] * 3,
        out_specs=(vmem,) * 5,
        scratch_shapes=[
            pltpu.VMEM((width, hidden), BF16),
            pltpu.VMEM((width, hidden), BF16),
            pltpu.VMEM((hidden, width), BF16),
            pltpu.VMEM((slots * blocks, LANES), F32),
            pltpu.VMEM((4, peers, cap * blocks, LANES), BF16),
            pltpu.VMEM((4, peers, cap * blocks, LANES), BF16),
            pltpu.VMEM((slots, width), BF16),
            pltpu.VMEM((slots, width), BF16),
            pltpu.VMEM((slots, hidden), F32),
            pltpu.VMEM((slots, hidden), F32),
            pltpu.VMEM((slots, hidden), BF16),
            pltpu.VMEM((slots, 2 * hidden), BF16),
            pltpu.VMEM((n_rep, own, 2 * hidden), BF16),
            pltpu.VMEM((n_rep, dn, width), BF16),
            pltpu.VMEM((2, half, own, 2 * hidden), BF16),
            pltpu.VMEM((2, half, dn, width), BF16),
            pltpu.VMEM((2, half - 1, own, 2 * hidden), BF16),
            pltpu.VMEM((2, half - 1, dn, width), BF16),
            pltpu.VMEM((2, n_rep, rows, own), BF16),
            pltpu.VMEM((2, n_rep, rows, own), BF16),
            dma((3,)), dma((4,)), dma((4,)), dma((2, 2, half)), dma((2, 2, half)),
            dma((2,)), dma((2,)),
        ],
        compiler_params=pltpu.CompilerParams(
            collective_id=0, has_side_effects=True, vmem_limit_bytes=48 * 1024 * 1024
        ),
        cost_estimate=pl.CostEstimate(
            flops=18 * slots * width * hidden, bytes_accessed=8 * width * hidden, transcendentals=0
        ),
    )(
        tokens, cotangent, routes, gate_weights,
        w_gate.reshape(width, hidden), w_up.reshape(width, hidden), w_down.reshape(hidden, width),
    )


def solution(mesh):
    at = ("outer", "inner")
    rows = P(at, None)
    pairs = P(at, "rep")
    weights = P(at, None, None)
    grads = P(at, "rep", None)
    return jax.shard_map(
        per_device,
        mesh=mesh,
        in_specs=(rows, rows, pairs, pairs, weights, weights, weights),
        out_specs=(pairs, pairs, grads, grads, grads),
        check_vma=False,
    )
```

```python
import functools

import jax
import jax.numpy as jnp
from jax import lax
from jax.experimental import pallas as pl
from jax.experimental.pallas import tpu as pltpu
from jax.sharding import PartitionSpec as P

MESH = pl.DeviceIdType.MESH
LANES = 128
F32 = jnp.float32
BF16 = jnp.bfloat16


def dot(a, b, dims=((1,), (0,))):
    return lax.dot_general(a, b, (dims, ((), ())), preferred_element_type=F32)


def kernel(
    sizes,
    tok_hbm, cot_hbm, routes_hbm, gate_hbm, wg_hbm, wu_hbm, wd_hbm,
    comb_ref, gtok_ref, gg_ref, gu_ref, gd_ref,
    tok, cot, routes, gate, wg, wu, wd, wide, send, recv, tok_in, sc_in, gpre, upre, hid, both,
    own_gu, own_dn, got_gu, got_dn, put_gu, put_dn, cols_out, cols_in, note, notes, pick,
    w_sem, a2a_send, a2a_recv, ch_send, ch_recv, rep_send, rep_recv,
):
    n_rep, n_out, n_in, cap = sizes
    peers = n_out * n_in
    rows, width = tok.shape
    blocks = width // LANES
    slots = peers * cap
    half = n_rep // 2
    r, o, i = lax.axis_index("rep"), lax.axis_index("outer"), lax.axis_index("inner")
    me = o * n_in + i

    operands = (
        (routes_hbm, routes), (tok_hbm, tok), (gate_hbm, gate), (cot_hbm, cot),
        (wg_hbm, wg), (wu_hbm, wu), (wd_hbm, wd),
    )
    loads = [pltpu.make_async_copy(a, b, w_sem.at[n]) for n, (a, b) in enumerate(operands)]
    for load in loads:
        load.start()

    barrier = pltpu.get_barrier_semaphore()

    def greet(k, c):
        o2, i2 = lax.rem(o + lax.div(k, n_in), n_out), lax.rem(i + lax.rem(k, n_in), n_in)
        pl.semaphore_signal(barrier, inc=1, device_id=(r, o2, i2), device_id_type=MESH)
        return c

    def greet_rep(k, c):
        pl.semaphore_signal(
            barrier, inc=1, device_id=(lax.rem(r + k, n_rep), o, i), device_id_type=MESH
        )
        return c

    lax.fori_loop(1, peers, greet, 0)
    lax.fori_loop(1, n_rep, greet_rep, 0)

    sub = lax.broadcasted_iota(jnp.int32, (rows, rows), 0)
    lane = lax.broadcasted_iota(jnp.int32, (rows, rows), 1)

    def column(row):
        return jnp.sum(jnp.where(sub == lane, row, 0.0), axis=1, keepdims=True)

    loads[0].wait()
    ids = routes[...].astype(F32)
    same = column(ids) == ids
    rank = jnp.sum(jnp.where(same & (sub < lane), 1.0, 0.0), axis=0, keepdims=True)
    slot = ids * float(cap) + rank
    place = lax.broadcasted_iota(jnp.int32, (slots, rows), 0).astype(F32)
    to_slots = jnp.where(place == slot, 1.0, 0.0).astype(BF16)

    def pack(rows_f32, n):
        for c in range(blocks):
            wide[pl.ds(c, slots, stride=blocks), :] = rows_f32(c)
        send[n] = wide[...].astype(BF16).reshape(peers, cap * blocks, LANES)
        recv[n, pl.ds(me, 1)] = send[n, pl.ds(me, 1)]

    def exchange(n):
        def one(k, c):
            m, di = lax.div(k, n_in), lax.rem(k, n_in)
            up, odd = lax.div(m + 1, 2), lax.rem(m, 2)
            do = odd * up + (1 - odd) * (n_out - up)
            o2, i2 = lax.rem(o + do, n_out), lax.rem(i + di, n_in)
            pltpu.make_async_remote_copy(
                src_ref=send.at[n, o2 * n_in + i2],
                dst_ref=recv.at[n, me],
                send_sem=a2a_send.at[n],
                recv_sem=a2a_recv.at[n],
                device_id=(r, o2, i2),
                device_id_type=MESH,
            ).start()
            return c

        lax.fori_loop(1, peers, one, 0)

    def arrive(n):
        got = recv.at[n, pl.ds(0, peers - 1)]
        pltpu.make_async_copy(got, got, a2a_recv.at[n]).wait()
        wide[...] = recv[n].reshape(slots * blocks, LANES).astype(F32)

    def block(c):
        return wide[pl.ds(c, slots, stride=blocks), :].astype(BF16)

    def unpack(n, dst):
        arrive(n)
        for c in range(blocks):
            dst[:, c * LANES : (c + 1) * LANES] = block(c)

    def spread(n, src, dst):
        def one(k, c):
            to = lax.rem(r + k, n_rep)
            pltpu.make_async_remote_copy(
                src_ref=src(to),
                dst_ref=dst.at[r],
                send_sem=rep_send.at[n],
                recv_sem=rep_recv.at[n],
                device_id=(to, o, i),
                device_id_type=MESH,
            ).start()
            return c

        lax.fori_loop(1, n_rep, one, 0)

    def spread_done(n, ref, sem):
        got = ref.at[pl.ds(0, n_rep - 1)]
        pltpu.make_async_copy(got, got, sem.at[n]).wait()

    def columns_out(n, rows_f32):
        for c in range(n_rep):
            cols_out[n, c] = rows_f32[:, c * LANES : (c + 1) * LANES].astype(BF16)
        cols_in[n, pl.ds(r, 1)] = cols_out[n, pl.ds(r, 1)]
        spread(n, lambda to: cols_out.at[n, to], cols_in.at[n])

    def columns_back(n):
        spread_done(n, cols_in.at[n], rep_recv)
        pack(lambda g: cols_in[n, g].astype(F32), 2 + n)
        exchange(2 + n)

    def columns_of(value):
        return lambda c: value[:, c * LANES : (c + 1) * LANES]

    loads[1].wait()
    pack(columns_of(dot(to_slots, tok[...])), 0)
    pl.semaphore_wait(barrier, peers - 1 + n_rep - 1)
    exchange(0)
    loads[2].wait()
    loads[3].wait()
    scaled = (column(gate[...]) * cot[...].astype(F32)).astype(BF16)
    pack(columns_of(dot(to_slots, scaled)), 1)
    exchange(1)

    note[...] = jnp.zeros_like(note)
    note[0:1, :] = slot
    note[1:2, :] = gate[...]
    notes[pl.ds(r, 1)] = note[...].reshape((1,) + note.shape)
    spread(2, lambda to: note, notes)

    for load in loads[4:]:
        load.wait()
    unpack(0, tok_in)
    gpre[...] = dot(tok_in[...], wg[...])
    upre[...] = dot(tok_in[...], wu[...])
    g = gpre[...]
    hid[...] = (g * jax.nn.sigmoid(g) * upre[...]).astype(BF16)
    columns_out(0, dot(hid[...], wd[...]))

    spread_done(2, notes, rep_recv)
    place_row = lax.broadcasted_iota(jnp.int32, (rows, slots), 1).astype(F32)
    for n in range(n_rep):
        pick[n] = jnp.where(place_row == column(notes[n, 0:1, :]), 1.0, 0.0).astype(BF16)
    columns_back(0)

    unpack(1, sc_in)
    hgrad = dot(sc_in[...], wd[...], ((1,), (1,)))
    g = gpre[...]
    s = jax.nn.sigmoid(g)
    f = g.shape[1]
    both[:, :f] = (hgrad * upre[...] * s * (1.0 + g * (1.0 - s))).astype(BF16)
    both[:, f:] = (hgrad * (g * s)).astype(BF16)
    columns_out(
        1, dot(both[:, :f], wg[...], ((1,), (1,))) + dot(both[:, f:], wu[...], ((1,), (1,)))
    )

    own_gu[...] = dot(tok_in[...], both[...], ((0,), (0,))).astype(BF16).reshape(own_gu.shape)
    own_dn[...] = dot(hid[...], sc_in[...], ((0,), (0,))).astype(BF16).reshape(own_dn.shape)

    pair = ((0, 1, own_gu, got_gu, put_gu), (1, 2, own_dn, got_dn, put_dn))

    def cut(a, side):
        ref = own_gu if a == 0 else own_dn
        if a == 0:
            n = ref.shape[1] // 2
            return (pl.ds(side * n, n), slice(None))
        n = ref.shape[2] // 2
        return (slice(None), pl.ds(side * n, n))

    def hop(a, d, t, src):
        got = pair[a][3]
        dst = got.at[d, t - 1]
        if t == half:
            src, dst = src.at[cut(a, d)], dst.at[cut(a, d)]
        to = lax.rem(r + (1 if d == 0 else n_rep - 1), n_rep)
        return pltpu.make_async_remote_copy(
            src_ref=src,
            dst_ref=dst,
            send_sem=ch_send.at[a, d, t - 1],
            recv_sem=ch_recv.at[a, d, t - 1],
            device_id=(to, o, i),
            device_id_type=MESH,
        )

    def owner(d, t):
        return lax.rem(r + (t if d == 0 else n_rep - t), n_rep)

    hops = {}
    for t in range(half, 0, -1):
        for a, unused, own, got, put in pair:
            for d in range(2):
                j = owner(d, t)
                if t == half:
                    src = own.at[j]
                else:
                    hops[a, d, t + 1].wait_recv()
                    if t + 1 == half:
                        x, y = cut(a, d), cut(a, 1 - d)
                        put[(d, t - 1) + x] = (
                            got[(d, t) + x].astype(F32) + own[(j,) + x].astype(F32)
                        ).astype(BF16)
                        put[(d, t - 1) + y] = own[(j,) + y]
                    else:
                        put[d, t - 1] = (got[d, t].astype(F32) + own[j].astype(F32)).astype(BF16)
                    src = put.at[d, t - 1]
                hops[a, d, t] = hop(a, d, t, src)
                hops[a, d, t].start()
        if t == half:
            columns_back(1)
    for a, unused, own, got, put in pair:
        for d in range(2):
            hops[a, d, 1].wait_recv()
        total = own[r].astype(F32) + got[0, 0].astype(F32) + got[1, 0].astype(F32)
        total = total.astype(BF16)
        if a == 0:
            gg_ref[0] = total[:, :f]
            gu_ref[0] = total[:, f:]
        else:
            gd_ref[0] = total

    def gather(n, weigh, out):
        arrive(2 + n)
        total = jnp.zeros((rows, LANES), F32)
        for c in range(n_rep):
            got = dot(pick[c], block(c))
            total += column(notes[c, 1:2, :]) * got if weigh else got
        out[...] = total.astype(BF16)

    gather(0, True, comb_ref)
    gather(1, False, gtok_ref)

    for n in range(4):
        sent = send.at[n, pl.ds(0, peers - 1)]
        pltpu.make_async_copy(sent, sent, a2a_send.at[n]).wait()
    spread_done(0, cols_out.at[0], rep_send)
    spread_done(1, cols_out.at[1], rep_send)
    spread_done(2, notes, rep_send)
    for h in hops.values():
        h.wait_send()


def deliver(*refs):
    n = len(refs) // 2
    for k in range(n):
        refs[n + k][...] = refs[k][...]


def per_device(tokens, cotangent, routes, gate_weights, w_gate, w_up, w_down):
    n_rep, n_out, n_in = (lax.axis_size(a) for a in ("rep", "outer", "inner"))
    rows, width = tokens.shape
    hidden = w_gate.shape[2]
    peers = n_out * n_in
    cap = max(2, 2 * rows // peers)
    blocks = width // LANES
    slots = peers * cap
    half = n_rep // 2
    own = width // n_rep
    dn = hidden // n_rep
    vmem = pl.BlockSpec(memory_space=pltpu.VMEM)
    hbm = pl.BlockSpec(memory_space=pl.ANY)
    dma = pltpu.SemaphoreType.DMA
    out_shape = (
        jax.ShapeDtypeStruct((rows, own), BF16),
        jax.ShapeDtypeStruct((rows, own), BF16),
        jax.ShapeDtypeStruct((1, own, hidden), BF16),
        jax.ShapeDtypeStruct((1, own, hidden), BF16),
        jax.ShapeDtypeStruct((1, dn, width), BF16),
    )
    results = pl.pallas_call(
        functools.partial(kernel, (n_rep, n_out, n_in, cap)),
        out_shape=out_shape,
        in_specs=[hbm] * 7,
        out_specs=(vmem,) * 5,
        scratch_shapes=[
            pltpu.VMEM((rows, width), BF16),
            pltpu.VMEM((rows, width), BF16),
            pltpu.VMEM((1, rows), jnp.int32),
            pltpu.VMEM((1, rows), F32),
            pltpu.VMEM((width, hidden), BF16),
            pltpu.VMEM((width, hidden), BF16),
            pltpu.VMEM((hidden, width), BF16),
            pltpu.VMEM((slots * blocks, LANES), F32),
            pltpu.VMEM((4, peers, cap * blocks, LANES), BF16),
            pltpu.VMEM((4, peers, cap * blocks, LANES), BF16),
            pltpu.VMEM((slots, width), BF16),
            pltpu.VMEM((slots, width), BF16),
            pltpu.VMEM((slots, hidden), F32),
            pltpu.VMEM((slots, hidden), F32),
            pltpu.VMEM((slots, hidden), BF16),
            pltpu.VMEM((slots, 2 * hidden), BF16),
            pltpu.VMEM((n_rep, own, 2 * hidden), BF16),
            pltpu.VMEM((n_rep, dn, width), BF16),
            pltpu.VMEM((2, half, own, 2 * hidden), BF16),
            pltpu.VMEM((2, half, dn, width), BF16),
            pltpu.VMEM((2, half - 1, own, 2 * hidden), BF16),
            pltpu.VMEM((2, half - 1, dn, width), BF16),
            pltpu.VMEM((2, n_rep, slots, LANES), BF16),
            pltpu.VMEM((2, n_rep, slots, LANES), BF16),
            pltpu.VMEM((8, rows), F32),
            pltpu.VMEM((n_rep, 8, rows), F32),
            pltpu.VMEM((n_rep, rows, slots), BF16),
            dma((7,)), dma((4,)), dma((4,)), dma((2, 2, half)), dma((2, 2, half)),
            dma((3,)), dma((3,)),
        ],
        compiler_params=pltpu.CompilerParams(
            collective_id=0, has_side_effects=True, vmem_limit_bytes=60 * 1024 * 1024
        ),
        cost_estimate=pl.CostEstimate(
            flops=18 * slots * width * hidden, bytes_accessed=8 * width * hidden, transcendentals=0
        ),
    )(
        tokens, cotangent, routes.reshape(1, rows), gate_weights.reshape(1, rows),
        w_gate.reshape(width, hidden), w_up.reshape(width, hidden), w_down.reshape(hidden, width),
    )
    return pl.pallas_call(
        deliver,
        out_shape=out_shape,
        in_specs=[vmem] * 5,
        out_specs=(vmem,) * 5,
    )(*results)


def solution(mesh):
    at = ("outer", "inner")
    rows = P(at, None)
    pairs = P(at, "rep")
    weights = P(at, None, None)
    grads = P(at, "rep", None)
    return jax.shard_map(
        per_device,
        mesh=mesh,
        in_specs=(rows, rows, pairs, pairs, weights, weights, weights),
        out_specs=(pairs, pairs, grads, grads, grads),
        check_vma=False,
    )
```

```python
import functools

import jax
import jax.numpy as jnp
from jax import lax
from jax.experimental import pallas as pl
from jax.experimental.pallas import tpu as pltpu
from jax.sharding import PartitionSpec as P

MESH = pl.DeviceIdType.MESH
LANES = 128
F32 = jnp.float32
BF16 = jnp.bfloat16


def dot(a, b, dims=((1,), (0,))):
    return lax.dot_general(a, b, (dims, ((), ())), preferred_element_type=F32)


def kernel(
    sizes,
    tok_hbm, cot_hbm, routes_hbm, gate_hbm, wg_hbm, wu_hbm, wd_hbm,
    comb_ref, gtok_ref, gg_ref, gu_ref, gd_ref,
    tok, cot, routes, gate, wg, wu, wd, wide, send, recv, tok_in, sc_in, gpre, upre, hid, both,
    own_gu, own_dn, got_gu, got_dn, put_gu, put_dn, cols_out, cols_in, note, notes, pick, pick_all,
    w_sem, a2a_send, a2a_recv, ch_send, ch_recv, rep_send, rep_recv,
):
    n_rep, n_out, n_in, cap = sizes
    peers = n_out * n_in
    rows, width = tok.shape
    blocks = width // LANES
    slots = peers * cap
    half = n_rep // 2
    r, o, i = lax.axis_index("rep"), lax.axis_index("outer"), lax.axis_index("inner")
    me = o * n_in + i

    operands = (
        (routes_hbm, routes), (tok_hbm, tok), (gate_hbm, gate), (cot_hbm, cot),
        (wg_hbm, wg), (wu_hbm, wu), (wd_hbm, wd),
    )
    loads = [pltpu.make_async_copy(a, b, w_sem.at[n]) for n, (a, b) in enumerate(operands)]
    for load in loads:
        load.start()

    barrier = pltpu.get_barrier_semaphore()

    inners = [i] + [lax.rem(i + k, n_in) for k in range(1, n_in)]

    def hello(r2, o2, i2):
        pl.semaphore_signal(barrier, inc=1, device_id=(r2, o2, i2), device_id_type=MESH)

    def greet(m, c):
        o2 = lax.rem(o + m, n_out)
        for i2 in inners:
            hello(r, o2, i2)
        return c

    for i2 in inners[1:]:
        hello(r, o, i2)
    lax.fori_loop(1, n_out, greet, 0)
    for k in range(1, n_rep):
        hello(lax.rem(r + k, n_rep), o, i)

    sub = lax.broadcasted_iota(jnp.int32, (rows, rows), 0)
    lane = lax.broadcasted_iota(jnp.int32, (rows, rows), 1)

    def column(row):
        return jnp.sum(jnp.where(sub == lane, row, 0.0), axis=1, keepdims=True)

    loads[0].wait()
    ids = routes[...].astype(F32)
    same = column(ids) == ids
    rank = jnp.sum(jnp.where(same & (sub < lane), 1.0, 0.0), axis=0, keepdims=True)
    slot = ids * float(cap) + rank
    place = lax.broadcasted_iota(jnp.int32, (slots, rows), 0).astype(F32)
    to_slots = jnp.where(place == slot, 1.0, 0.0).astype(BF16)

    def pack(rows_f32, n):
        for c in range(blocks):
            wide[pl.ds(c, slots, stride=blocks), :] = rows_f32(c)
        send[n] = wide[...].astype(BF16).reshape(peers, cap * blocks, LANES)
        recv[n, pl.ds(me, 1)] = send[n, pl.ds(me, 1)]

    def exchange(n):
        def one(o2, i2):
            pltpu.make_async_remote_copy(
                src_ref=send.at[n, o2 * n_in + i2],
                dst_ref=recv.at[n, me],
                send_sem=a2a_send.at[n],
                recv_sem=a2a_recv.at[n],
                device_id=(r, o2, i2),
                device_id_type=MESH,
            ).start()

        def plane(m, c):
            up, odd = lax.div(m + 1, 2), lax.rem(m, 2)
            o2 = lax.rem(o + odd * up + (1 - odd) * (n_out - up), n_out)
            for i2 in inners:
                one(o2, i2)
            return c

        for i2 in inners[1:]:
            one(o, i2)
        lax.fori_loop(1, n_out, plane, 0)

    def landed(n):
        got = recv.at[n, pl.ds(0, peers - 1)]
        pltpu.make_async_copy(got, got, a2a_recv.at[n]).wait()

    def arrive(n):
        landed(n)
        wide[...] = recv[n].reshape(slots * blocks, LANES).astype(F32)

    def block(c):
        return wide[pl.ds(c, slots, stride=blocks), :].astype(BF16)

    def unpack(n, dst):
        arrive(n)
        for c in range(blocks):
            dst[:, c * LANES : (c + 1) * LANES] = block(c)

    def spread(n, src, dst):
        def one(k, c):
            to = lax.rem(r + k, n_rep)
            pltpu.make_async_remote_copy(
                src_ref=src(to),
                dst_ref=dst.at[r],
                send_sem=rep_send.at[n],
                recv_sem=rep_recv.at[n],
                device_id=(to, o, i),
                device_id_type=MESH,
            ).start()
            return c

        lax.fori_loop(1, n_rep, one, 0)

    def spread_done(n, ref, sem):
        got = ref.at[pl.ds(0, n_rep - 1)]
        pltpu.make_async_copy(got, got, sem.at[n]).wait()

    def columns_out(n, rows_f32):
        for c in range(n_rep):
            cols_out[n, c] = rows_f32[:, c * LANES : (c + 1) * LANES].astype(BF16)
        cols_in[n, pl.ds(r, 1)] = cols_out[n, pl.ds(r, 1)]
        spread(n, lambda to: cols_out.at[n, to], cols_in.at[n])

    def columns_back(n):
        spread_done(n, cols_in.at[n], rep_recv)
        pack(lambda g: cols_in[n, g].astype(F32), 2 + n)
        exchange(2 + n)

    def columns_of(value):
        return lambda c: value[:, c * LANES : (c + 1) * LANES]

    loads[1].wait()
    pack(columns_of(dot(to_slots, tok[...])), 0)
    pl.semaphore_wait(barrier, peers - 1 + n_rep - 1)
    exchange(0)
    loads[2].wait()
    loads[3].wait()
    scaled = (column(gate[...]) * cot[...].astype(F32)).astype(BF16)
    pack(columns_of(dot(to_slots, scaled)), 1)
    exchange(1)

    note[...] = jnp.zeros_like(note)
    note[0:1, :] = slot
    note[1:2, :] = gate[...]
    notes[pl.ds(r, 1)] = note[...].reshape((1,) + note.shape)
    spread(2, lambda to: note, notes)

    for load in loads[4:]:
        load.wait()
    unpack(0, tok_in)
    gpre[...] = dot(tok_in[...], wg[...])
    upre[...] = dot(tok_in[...], wu[...])
    g = gpre[...]
    hid[...] = (g * jax.nn.sigmoid(g) * upre[...]).astype(BF16)
    columns_out(0, dot(hid[...], wd[...]))

    spread_done(2, notes, rep_recv)
    place_row = lax.broadcasted_iota(jnp.int32, (rows, slots), 1).astype(F32)
    for n in range(n_rep):
        pick[n] = jnp.where(place_row == column(notes[n, 0:1, :]), 1.0, 0.0).astype(BF16)
    columns_back(0)

    table = jnp.concatenate([notes[n, 0:1, :] for n in range(n_rep)], axis=0).astype(BF16)
    group = lax.broadcasted_iota(jnp.int32, (n_rep, LANES), 0)
    of_lane = lax.rem(lax.broadcasted_iota(jnp.int32, (n_rep, LANES), 1), n_rep)
    spread_slots = dot(table, jnp.where(group == of_lane, 1.0, 0.0).astype(BF16), ((0,), (0,)))
    at_lane = lax.div(lax.broadcasted_iota(jnp.int32, (rows, LANES), 1), n_rep)
    for n in range(slots * n_rep // LANES):
        target = (at_lane + n * (LANES // n_rep)).astype(F32)
        pick_all[:, n * LANES : (n + 1) * LANES] = jnp.where(
            spread_slots == target, 1.0, 0.0
        ).astype(BF16)

    g = gpre[...]
    s = jax.nn.sigmoid(g)
    f = g.shape[1]
    gpre[...] = upre[...] * s * (1.0 + g * (1.0 - s))
    upre[...] = g * s
    unpack(1, sc_in)
    hgrad = dot(sc_in[...], wd[...], ((1,), (1,)))
    both[:, :f] = (hgrad * gpre[...]).astype(BF16)
    both[:, f:] = (hgrad * upre[...]).astype(BF16)
    for k in range(1, n_rep + 1):
        c = lax.rem(r + k, n_rep)
        at = pl.ds(pl.multiple_of(c * LANES, LANES), LANES)
        rows_f32 = dot(both[:, :f], wg[at, :], ((1,), (1,)))
        rows_f32 += dot(both[:, f:], wu[at, :], ((1,), (1,)))
        if k == n_rep:
            cols_in[1, pl.ds(c, 1)] = rows_f32.astype(BF16).reshape(1, slots, LANES)
        else:
            cols_out[1, pl.ds(c, 1)] = rows_f32.astype(BF16).reshape(1, slots, LANES)
            pltpu.make_async_remote_copy(
                src_ref=cols_out.at[1, c],
                dst_ref=cols_in.at[1, r],
                send_sem=rep_send.at[1],
                recv_sem=rep_recv.at[1],
                device_id=(c, o, i),
                device_id_type=MESH,
            ).start()

    own_gu[...] = dot(tok_in[...], both[...], ((0,), (0,))).astype(BF16).reshape(own_gu.shape)
    own_dn[...] = dot(hid[...], sc_in[...], ((0,), (0,))).astype(BF16).reshape(own_dn.shape)

    pair = ((0, 1, own_gu, got_gu, put_gu), (1, 2, own_dn, got_dn, put_dn))

    def cut(a, side):
        ref = own_gu if a == 0 else own_dn
        if a == 0:
            n = ref.shape[1] // 2
            return (pl.ds(side * n, n), slice(None))
        n = ref.shape[2] // 2
        return (slice(None), pl.ds(side * n, n))

    def hop(a, d, t, src):
        got = pair[a][3]
        dst = got.at[d, t - 1]
        if t == half:
            src, dst = src.at[cut(a, d)], dst.at[cut(a, d)]
        to = lax.rem(r + (1 if d == 0 else n_rep - 1), n_rep)
        return pltpu.make_async_remote_copy(
            src_ref=src,
            dst_ref=dst,
            send_sem=ch_send.at[a, d, t - 1],
            recv_sem=ch_recv.at[a, d, t - 1],
            device_id=(to, o, i),
            device_id_type=MESH,
        )

    def owner(d, t):
        return lax.rem(r + (t if d == 0 else n_rep - t), n_rep)

    columns_back(1)
    hops = {}
    for t in range(half, 0, -1):
        for a, unused, own, got, put in pair:
            for d in range(2):
                j = owner(d, t)
                if t == half:
                    src = own.at[j]
                else:
                    hops[a, d, t + 1].wait_recv()
                    if t + 1 == half:
                        x, y = cut(a, d), cut(a, 1 - d)
                        put[(d, t - 1) + x] = (
                            got[(d, t) + x].astype(F32) + own[(j,) + x].astype(F32)
                        ).astype(BF16)
                        put[(d, t - 1) + y] = own[(j,) + y]
                    else:
                        put[d, t - 1] = (got[d, t].astype(F32) + own[j].astype(F32)).astype(BF16)
                    src = put.at[d, t - 1]
                hops[a, d, t] = hop(a, d, t, src)
                hops[a, d, t].start()
    for a, unused, own, got, put in pair:
        for d in range(2):
            hops[a, d, 1].wait_recv()
        total = own[r].astype(F32) + got[0, 0].astype(F32) + got[1, 0].astype(F32)
        total = total.astype(BF16)
        if a == 0:
            gg_ref[0] = total[:, :f]
            gu_ref[0] = total[:, f:]
        else:
            gd_ref[0] = total

    arrive(2)
    total = jnp.zeros((rows, LANES), F32)
    for c in range(n_rep):
        total += column(notes[c, 1:2, :]) * dot(pick[c], block(c))
    comb_ref[...] = total.astype(BF16)
    landed(3)
    gtok_ref[...] = dot(pick_all[...], recv[3].reshape(slots * n_rep, LANES)).astype(BF16)

    for n in range(4):
        sent = send.at[n, pl.ds(0, peers - 1)]
        pltpu.make_async_copy(sent, sent, a2a_send.at[n]).wait()
    spread_done(0, cols_out.at[0], rep_send)
    spread_done(1, cols_out.at[1], rep_send)
    spread_done(2, notes, rep_send)
    for h in hops.values():
        h.wait_send()


def deliver(*refs):
    n = len(refs) // 2
    for k in range(n):
        refs[n + k][...] = refs[k][...]


def per_device(tokens, cotangent, routes, gate_weights, w_gate, w_up, w_down):
    n_rep, n_out, n_in = (lax.axis_size(a) for a in ("rep", "outer", "inner"))
    rows, width = tokens.shape
    hidden = w_gate.shape[2]
    peers = n_out * n_in
    cap = max(2, 2 * rows // peers)
    blocks = width // LANES
    slots = peers * cap
    half = n_rep // 2
    own = width // n_rep
    dn = hidden // n_rep
    vmem = pl.BlockSpec(memory_space=pltpu.VMEM)
    hbm = pl.BlockSpec(memory_space=pl.ANY)
    dma = pltpu.SemaphoreType.DMA
    out_shape = (
        jax.ShapeDtypeStruct((rows, own), BF16),
        jax.ShapeDtypeStruct((rows, own), BF16),
        jax.ShapeDtypeStruct((1, own, hidden), BF16),
        jax.ShapeDtypeStruct((1, own, hidden), BF16),
        jax.ShapeDtypeStruct((1, dn, width), BF16),
    )
    results = pl.pallas_call(
        functools.partial(kernel, (n_rep, n_out, n_in, cap)),
        out_shape=out_shape,
        in_specs=[hbm] * 7,
        out_specs=(vmem,) * 5,
        scratch_shapes=[
            pltpu.VMEM((rows, width), BF16),
            pltpu.VMEM((rows, width), BF16),
            pltpu.VMEM((1, rows), jnp.int32),
            pltpu.VMEM((1, rows), F32),
            pltpu.VMEM((width, hidden), BF16),
            pltpu.VMEM((width, hidden), BF16),
            pltpu.VMEM((hidden, width), BF16),
            pltpu.VMEM((slots * blocks, LANES), F32),
            pltpu.VMEM((4, peers, cap * blocks, LANES), BF16),
            pltpu.VMEM((4, peers, cap * blocks, LANES), BF16),
            pltpu.VMEM((slots, width), BF16),
            pltpu.VMEM((slots, width), BF16),
            pltpu.VMEM((slots, hidden), F32),
            pltpu.VMEM((slots, hidden), F32),
            pltpu.VMEM((slots, hidden), BF16),
            pltpu.VMEM((slots, 2 * hidden), BF16),
            pltpu.VMEM((n_rep, own, 2 * hidden), BF16),
            pltpu.VMEM((n_rep, dn, width), BF16),
            pltpu.VMEM((2, half, own, 2 * hidden), BF16),
            pltpu.VMEM((2, half, dn, width), BF16),
            pltpu.VMEM((2, half - 1, own, 2 * hidden), BF16),
            pltpu.VMEM((2, half - 1, dn, width), BF16),
            pltpu.VMEM((2, n_rep, slots, LANES), BF16),
            pltpu.VMEM((2, n_rep, slots, LANES), BF16),
            pltpu.VMEM((8, rows), F32),
            pltpu.VMEM((n_rep, 8, rows), F32),
            pltpu.VMEM((n_rep, rows, slots), BF16),
            pltpu.VMEM((rows, slots * n_rep), BF16),
            dma((7,)), dma((4,)), dma((4,)), dma((2, 2, half)), dma((2, 2, half)),
            dma((3,)), dma((3,)),
        ],
        compiler_params=pltpu.CompilerParams(
            collective_id=0, has_side_effects=True, vmem_limit_bytes=60 * 1024 * 1024
        ),
        cost_estimate=pl.CostEstimate(
            flops=18 * slots * width * hidden, bytes_accessed=8 * width * hidden, transcendentals=0
        ),
    )(
        tokens, cotangent, routes.reshape(1, rows), gate_weights.reshape(1, rows),
        w_gate.reshape(width, hidden), w_up.reshape(width, hidden), w_down.reshape(hidden, width),
    )
    return pl.pallas_call(
        deliver,
        out_shape=out_shape,
        in_specs=[vmem] * 5,
        out_specs=(vmem,) * 5,
    )(*results)


def solution(mesh):
    at = ("outer", "inner")
    rows = P(at, None)
    pairs = P(at, "rep")
    weights = P(at, None, None)
    grads = P(at, "rep", None)
    return jax.shard_map(
        per_device,
        mesh=mesh,
        in_specs=(rows, rows, pairs, pairs, weights, weights, weights),
        out_specs=(pairs, pairs, grads, grads, grads),
        check_vma=False,
    )
```

```python
import functools

import jax
import jax.numpy as jnp
from jax import lax
from jax.experimental import pallas as pl
from jax.experimental.pallas import tpu as pltpu
from jax.sharding import PartitionSpec as P

MESH = pl.DeviceIdType.MESH
LANES = 128
F32 = jnp.float32
BF16 = jnp.bfloat16


def dot(a, b, dims=((1,), (0,))):
    return lax.dot_general(a, b, (dims, ((), ())), preferred_element_type=F32)


def kernel(
    sizes,
    tok_hbm, cot_hbm, routes_hbm, gate_hbm, wg_hbm, wu_hbm, wd_hbm,
    comb_ref, gtok_ref, gg_ref, gu_ref, gd_ref,
    tok, cot, routes, gate, wg, wu, wd, wide, send, recv, tok_in, sc_in, gpre, upre, hid, both,
    own_gu, own_dn, got_gu, got_dn, put_gu, put_dn, cols_out, cols_in, note, notes, pick, pick_all,
    w_sem, a2a_send, a2a_recv, ch_send, ch_recv, rep_send, rep_recv,
):
    n_rep, n_out, n_in, cap = sizes
    peers = n_out * n_in
    rows, width = tok.shape
    blocks = width // LANES
    slots = peers * cap
    half = n_rep // 2
    r, o, i = lax.axis_index("rep"), lax.axis_index("outer"), lax.axis_index("inner")
    me = o * n_in + i

    operands = (
        (routes_hbm, routes), (tok_hbm, tok), (gate_hbm, gate), (cot_hbm, cot),
        (wg_hbm, wg), (wu_hbm, wu), (wd_hbm, wd),
    )
    loads = [pltpu.make_async_copy(a, b, w_sem.at[n]) for n, (a, b) in enumerate(operands)]
    for load in loads:
        load.start()

    barrier = pltpu.get_barrier_semaphore()

    inners = [i] + [lax.rem(i + k, n_in) for k in range(1, n_in)]

    def hello(r2, o2, i2):
        pl.semaphore_signal(barrier, inc=1, device_id=(r2, o2, i2), device_id_type=MESH)

    def greet(m, c):
        o2 = lax.rem(o + m, n_out)
        for i2 in inners:
            hello(r, o2, i2)
        return c

    for i2 in inners[1:]:
        hello(r, o, i2)
    lax.fori_loop(1, n_out, greet, 0)
    for k in range(1, n_rep):
        hello(lax.rem(r + k, n_rep), o, i)

    sub = lax.broadcasted_iota(jnp.int32, (rows, rows), 0)
    lane = lax.broadcasted_iota(jnp.int32, (rows, rows), 1)

    def column(row):
        return jnp.sum(jnp.where(sub == lane, row, 0.0), axis=1, keepdims=True)

    loads[0].wait()
    ids = routes[...].astype(F32)
    same = column(ids) == ids
    rank = jnp.sum(jnp.where(same & (sub < lane), 1.0, 0.0), axis=0, keepdims=True)
    slot = ids * float(cap) + rank
    place = lax.broadcasted_iota(jnp.int32, (slots, rows), 0).astype(F32)
    to_slots = jnp.where(place == slot, 1.0, 0.0).astype(BF16)

    def pack(rows_f32, n):
        for c in range(blocks):
            wide[pl.ds(c, slots, stride=blocks), :] = rows_f32(c)
        send[n] = wide[...].astype(BF16).reshape(peers, cap * blocks, LANES)
        recv[n, pl.ds(me, 1)] = send[n, pl.ds(me, 1)]

    def exchange(n):
        def one(o2, i2):
            pltpu.make_async_remote_copy(
                src_ref=send.at[n, o2 * n_in + i2],
                dst_ref=recv.at[n, me],
                send_sem=a2a_send.at[n],
                recv_sem=a2a_recv.at[n],
                device_id=(r, o2, i2),
                device_id_type=MESH,
            ).start()

        def plane(m, c):
            up, odd = lax.div(m + 1, 2), lax.rem(m, 2)
            o2 = lax.rem(o + odd * up + (1 - odd) * (n_out - up), n_out)
            for i2 in inners:
                one(o2, i2)
            return c

        for i2 in inners[1:]:
            one(o, i2)
        lax.fori_loop(1, n_out, plane, 0)

    def landed(n):
        got = recv.at[n, pl.ds(0, peers - 1)]
        pltpu.make_async_copy(got, got, a2a_recv.at[n]).wait()

    def arrive(n):
        landed(n)
        wide[...] = recv[n].reshape(slots * blocks, LANES).astype(F32)

    def block(c):
        return wide[pl.ds(c, slots, stride=blocks), :].astype(BF16)

    def unpack(n, dst):
        arrive(n)
        for c in range(blocks):
            dst[:, c * LANES : (c + 1) * LANES] = block(c)

    def spread(n, src, dst):
        def one(k, c):
            to = lax.rem(r + k, n_rep)
            pltpu.make_async_remote_copy(
                src_ref=src(to),
                dst_ref=dst.at[r],
                send_sem=rep_send.at[n],
                recv_sem=rep_recv.at[n],
                device_id=(to, o, i),
                device_id_type=MESH,
            ).start()
            return c

        lax.fori_loop(1, n_rep, one, 0)

    def spread_done(n, ref, sem):
        got = ref.at[pl.ds(0, n_rep - 1)]
        pltpu.make_async_copy(got, got, sem.at[n]).wait()

    def columns_out(n, rows_f32):
        for c in range(n_rep):
            cols_out[n, c] = rows_f32[:, c * LANES : (c + 1) * LANES].astype(BF16)
        cols_in[n, pl.ds(r, 1)] = cols_out[n, pl.ds(r, 1)]
        spread(n, lambda to: cols_out.at[n, to], cols_in.at[n])

    def columns_back(n):
        spread_done(n, cols_in.at[n], rep_recv)
        pack(lambda g: cols_in[n, g].astype(F32), 2 + n)
        exchange(2 + n)

    def columns_of(value):
        return lambda c: value[:, c * LANES : (c + 1) * LANES]

    loads[1].wait()
    pack(columns_of(dot(to_slots, tok[...])), 0)
    pl.semaphore_wait(barrier, peers - 1 + n_rep - 1)
    exchange(0)
    loads[2].wait()
    loads[3].wait()
    scaled = (column(gate[...]) * cot[...].astype(F32)).astype(BF16)
    pack(columns_of(dot(to_slots, scaled)), 1)
    exchange(1)

    note[...] = jnp.zeros_like(note)
    note[0:1, :] = slot
    note[1:2, :] = gate[...]
    notes[pl.ds(r, 1)] = note[...].reshape((1,) + note.shape)
    spread(2, lambda to: note, notes)

    for load in loads[4:]:
        load.wait()
    unpack(0, tok_in)
    gpre[...] = dot(tok_in[...], wg[...])
    upre[...] = dot(tok_in[...], wu[...])
    g = gpre[...]
    hid[...] = (g * jax.nn.sigmoid(g) * upre[...]).astype(BF16)
    columns_out(0, dot(hid[...], wd[...]))

    spread_done(2, notes, rep_recv)
    place_row = lax.broadcasted_iota(jnp.int32, (rows, slots), 1).astype(F32)
    for n in range(n_rep):
        pick[n] = jnp.where(place_row == column(notes[n, 0:1, :]), 1.0, 0.0).astype(BF16)
    columns_back(0)

    table = jnp.concatenate([notes[n, 0:1, :] for n in range(n_rep)], axis=0).astype(BF16)
    group = lax.broadcasted_iota(jnp.int32, (n_rep, LANES), 0)
    of_lane = lax.rem(lax.broadcasted_iota(jnp.int32, (n_rep, LANES), 1), n_rep)
    spread_slots = dot(table, jnp.where(group == of_lane, 1.0, 0.0).astype(BF16), ((0,), (0,)))
    at_lane = lax.div(lax.broadcasted_iota(jnp.int32, (rows, LANES), 1), n_rep)
    for n in range(slots * n_rep // LANES):
        target = (at_lane + n * (LANES // n_rep)).astype(F32)
        pick_all[:, n * LANES : (n + 1) * LANES] = jnp.where(
            spread_slots == target, 1.0, 0.0
        ).astype(BF16)

    g = gpre[...]
    s = jax.nn.sigmoid(g)
    f = g.shape[1]
    gpre[...] = upre[...] * s * (1.0 + g * (1.0 - s))
    upre[...] = g * s
    unpack(1, sc_in)
    hgrad = dot(sc_in[...], wd[...], ((1,), (1,)))
    both[:, :f] = (hgrad * gpre[...]).astype(BF16)
    both[:, f:] = (hgrad * upre[...]).astype(BF16)
    for k in range(1, n_rep + 1):
        c = lax.rem(r + k, n_rep)
        at = pl.ds(pl.multiple_of(c * LANES, LANES), LANES)
        rows_f32 = dot(both[:, :f], wg[at, :], ((1,), (1,)))
        rows_f32 += dot(both[:, f:], wu[at, :], ((1,), (1,)))
        if k == n_rep:
            cols_in[1, pl.ds(c, 1)] = rows_f32.astype(BF16).reshape(1, slots, LANES)
        else:
            cols_out[1, pl.ds(c, 1)] = rows_f32.astype(BF16).reshape(1, slots, LANES)
            pltpu.make_async_remote_copy(
                src_ref=cols_out.at[1, c],
                dst_ref=cols_in.at[1, r],
                send_sem=rep_send.at[1],
                recv_sem=rep_recv.at[1],
                device_id=(c, o, i),
                device_id_type=MESH,
            ).start()

    own_gu[...] = dot(tok_in[...], both[...], ((0,), (0,))).astype(BF16).reshape(own_gu.shape)
    own_dn[...] = dot(hid[...], sc_in[...], ((0,), (0,))).astype(BF16).reshape(own_dn.shape)

    pair = ((0, 1, own_gu, got_gu, put_gu), (1, 2, own_dn, got_dn, put_dn))

    def cut(a, side):
        ref = own_gu if a == 0 else own_dn
        if a == 0:
            n = ref.shape[1] // 2
            return (pl.ds(side * n, n), slice(None))
        n = ref.shape[2] // 2
        return (slice(None), pl.ds(side * n, n))

    def hop(a, d, t, src):
        got = pair[a][3]
        dst = got.at[d, t - 1]
        if t == half:
            src, dst = src.at[cut(a, d)], dst.at[cut(a, d)]
        to = lax.rem(r + (1 if d == 0 else n_rep - 1), n_rep)
        return pltpu.make_async_remote_copy(
            src_ref=src,
            dst_ref=dst,
            send_sem=ch_send.at[a, d, t - 1],
            recv_sem=ch_recv.at[a, d, t - 1],
            device_id=(to, o, i),
            device_id_type=MESH,
        )

    def owner(d, t):
        return lax.rem(r + (t if d == 0 else n_rep - t), n_rep)

    hops = {}
    for t in range(half, 0, -1):
        for a, unused, own, got, put in pair:
            for d in range(2):
                j = owner(d, t)
                if t == half:
                    src = own.at[j]
                else:
                    hops[a, d, t + 1].wait_recv()
                    if t + 1 == half:
                        x, y = cut(a, d), cut(a, 1 - d)
                        put[(d, t - 1) + x] = (
                            got[(d, t) + x].astype(F32) + own[(j,) + x].astype(F32)
                        ).astype(BF16)
                        put[(d, t - 1) + y] = own[(j,) + y]
                    else:
                        put[d, t - 1] = (got[d, t].astype(F32) + own[j].astype(F32)).astype(BF16)
                    src = put.at[d, t - 1]
                hops[a, d, t] = hop(a, d, t, src)
                hops[a, d, t].start()
        if t == half:
            columns_back(1)
    for a, unused, own, got, put in pair:
        for d in range(2):
            hops[a, d, 1].wait_recv()
        total = own[r].astype(F32) + got[0, 0].astype(F32) + got[1, 0].astype(F32)
        total = total.astype(BF16)
        if a == 0:
            gg_ref[0] = total[:, :f]
            gu_ref[0] = total[:, f:]
        else:
            gd_ref[0] = total

    arrive(2)
    total = jnp.zeros((rows, LANES), F32)
    for c in range(n_rep):
        total += column(notes[c, 1:2, :]) * dot(pick[c], block(c))
    comb_ref[...] = total.astype(BF16)
    landed(3)
    gtok_ref[...] = dot(pick_all[...], recv[3].reshape(slots * n_rep, LANES)).astype(BF16)

    for n in range(4):
        sent = send.at[n, pl.ds(0, peers - 1)]
        pltpu.make_async_copy(sent, sent, a2a_send.at[n]).wait()
    spread_done(0, cols_out.at[0], rep_send)
    spread_done(1, cols_out.at[1], rep_send)
    spread_done(2, notes, rep_send)
    for h in hops.values():
        h.wait_send()


def deliver(*refs):
    n = len(refs) // 2
    for k in range(n):
        refs[n + k][...] = refs[k][...]


def per_device(tokens, cotangent, routes, gate_weights, w_gate, w_up, w_down):
    n_rep, n_out, n_in = (lax.axis_size(a) for a in ("rep", "outer", "inner"))
    rows, width = tokens.shape
    hidden = w_gate.shape[2]
    peers = n_out * n_in
    cap = max(2, 2 * rows // peers)
    blocks = width // LANES
    slots = peers * cap
    half = n_rep // 2
    own = width // n_rep
    dn = hidden // n_rep
    vmem = pl.BlockSpec(memory_space=pltpu.VMEM)
    hbm = pl.BlockSpec(memory_space=pl.ANY)
    dma = pltpu.SemaphoreType.DMA
    out_shape = (
        jax.ShapeDtypeStruct((rows, own), BF16),
        jax.ShapeDtypeStruct((rows, own), BF16),
        jax.ShapeDtypeStruct((1, own, hidden), BF16),
        jax.ShapeDtypeStruct((1, own, hidden), BF16),
        jax.ShapeDtypeStruct((1, dn, width), BF16),
    )
    results = pl.pallas_call(
        functools.partial(kernel, (n_rep, n_out, n_in, cap)),
        out_shape=out_shape,
        in_specs=[hbm] * 7,
        out_specs=(vmem,) * 5,
        scratch_shapes=[
            pltpu.VMEM((rows, width), BF16),
            pltpu.VMEM((rows, width), BF16),
            pltpu.VMEM((1, rows), jnp.int32),
            pltpu.VMEM((1, rows), F32),
            pltpu.VMEM((width, hidden), BF16),
            pltpu.VMEM((width, hidden), BF16),
            pltpu.VMEM((hidden, width), BF16),
            pltpu.VMEM((slots * blocks, LANES), F32),
            pltpu.VMEM((4, peers, cap * blocks, LANES), BF16),
            pltpu.VMEM((4, peers, cap * blocks, LANES), BF16),
            pltpu.VMEM((slots, width), BF16),
            pltpu.VMEM((slots, width), BF16),
            pltpu.VMEM((slots, hidden), F32),
            pltpu.VMEM((slots, hidden), F32),
            pltpu.VMEM((slots, hidden), BF16),
            pltpu.VMEM((slots, 2 * hidden), BF16),
            pltpu.VMEM((n_rep, own, 2 * hidden), BF16),
            pltpu.VMEM((n_rep, dn, width), BF16),
            pltpu.VMEM((2, half, own, 2 * hidden), BF16),
            pltpu.VMEM((2, half, dn, width), BF16),
            pltpu.VMEM((2, half - 1, own, 2 * hidden), BF16),
            pltpu.VMEM((2, half - 1, dn, width), BF16),
            pltpu.VMEM((2, n_rep, slots, LANES), BF16),
            pltpu.VMEM((2, n_rep, slots, LANES), BF16),
            pltpu.VMEM((8, rows), F32),
            pltpu.VMEM((n_rep, 8, rows), F32),
            pltpu.VMEM((n_rep, rows, slots), BF16),
            pltpu.VMEM((rows, slots * n_rep), BF16),
            dma((7,)), dma((4,)), dma((4,)), dma((2, 2, half)), dma((2, 2, half)),
            dma((3,)), dma((3,)),
        ],
        compiler_params=pltpu.CompilerParams(
            collective_id=0, has_side_effects=True, vmem_limit_bytes=60 * 1024 * 1024
        ),
        cost_estimate=pl.CostEstimate(
            flops=18 * slots * width * hidden, bytes_accessed=8 * width * hidden, transcendentals=0
        ),
    )(
        tokens, cotangent, routes.reshape(1, rows), gate_weights.reshape(1, rows),
        w_gate.reshape(width, hidden), w_up.reshape(width, hidden), w_down.reshape(hidden, width),
    )
    return pl.pallas_call(
        deliver,
        out_shape=out_shape,
        in_specs=[vmem] * 5,
        out_specs=(vmem,) * 5,
    )(*results)


def solution(mesh):
    at = ("outer", "inner")
    rows = P(at, None)
    pairs = P(at, "rep")
    weights = P(at, None, None)
    grads = P(at, "rep", None)
    return jax.shard_map(
        per_device,
        mesh=mesh,
        in_specs=(rows, rows, pairs, pairs, weights, weights, weights),
        out_specs=(pairs, pairs, grads, grads, grads),
        check_vma=False,
    )
```
